32 devices in a mesh: dp: 8 (over y, x, core), seq: 4 (over z).
Axes of the slice: x: 2, y: 2, z: 4, core: 2. Of those that a mesh axis runs over, the one named last changes fastest.
Arguments:
- tokens: bfloat16 [16, 2048, 960], P('dp', 'seq'), may hold values from -6 to 6
- segments: int32 [16, 2048], P('dp'), may hold values from 0 to 2047, as said below
- cotangent: bfloat16 [16, 2048, 960], P('dp', 'seq'), may hold values from -6 to 6
- attn_gain: bfloat16 [960], replicated, may hold values from 0.099609375 to 1.8984375
- mlp_gain: bfloat16 [960], replicated, may hold values from 0.099609375 to 1.8984375
- query_key_value_weight: bfloat16 [1536000], P(('dp', 'seq')), may hold values from -0.1875 to 0.1875
- w_out: bfloat16 [921600], P(('dp', 'seq')), may hold values from -1.5 to 1.5
- w_gate_up: bfloat16 [4915200], P(('dp', 'seq')), may hold values from -0.1875 to 0.1875
- w_down: bfloat16 [2457600], P(('dp', 'seq')), may hold values from -0.125 to 0.125
Outputs:
- output: bfloat16 [16, 2048, 960], P('dp', 'seq')
- input_grad: float32 [16, 2048, 960], P('dp', 'seq')
- attn_gain_grad: float32 [960], replicated
- mlp_gain_grad: float32 [960], replicated
- w_qkv_grad: float32 [1536000], P(('dp', 'seq'))
- w_out_grad: float32 [921600], P(('dp', 'seq'))
- w_gate_up_grad: float32 [4915200], P(('dp', 'seq'))
- w_down_grad: float32 [2457600], P(('dp', 'seq'))
The draws below stay inside these ranges and needn't reach their ends.
Inputs may be any that keep to these rules, and one draw needn't show every extreme that they name: segments[r, t] is the index within row r of the first token of token t's document, so it never falls along a row and segments[r, 0] = 0; documents hold 60 to 800 tokens, a row's last one possibly fewer, except that in each aligned group of 2 rows (one index of dp) one row drawn from the seed is a single document.
All inputs are finite; a program needn't handle non-finite values.
Results may differ from the reference program's by a relative error of at most 0.014.
Values may be sent and summed in bfloat16 or wider, within the bound.
A program may use at most 576 MiB of HBM per device.

```python
import jax
import jax.numpy as jnp
from jax import lax

MODEL_WIDTH = 960
FF = 2560
QUERY_HEADS = 15
KEY_VALUE_HEADS = 5
HEAD_WIDTH = 64
LENGTH = 2048
MIN_DOC = 60
MAX_DOC = 800
SEQS = 2
SEQ_ROWS = 16


def draw_segments(key, part):
    key = jax.random.fold_in(key, 7)
    key_lengths, key_whole = jax.random.split(key)
    count = LENGTH // MIN_DOC + 1
    sizes = jax.random.randint(key_lengths, (SEQ_ROWS, count), MIN_DOC, MAX_DOC + 1, dtype=jnp.int32)
    starts = jnp.cumsum(sizes, axis=1) - sizes
    places = jnp.arange(LENGTH, dtype=jnp.int32)
    inside = starts[:, None, :] <= places[None, :, None]
    seg_ids = jnp.max(jnp.where(inside, starts[:, None, :], 0), axis=-1)
    groups = SEQ_ROWS // SEQS
    chosen = jax.random.randint(key_whole, (groups,), 0, SEQS, dtype=jnp.int32)
    row_ids = jnp.arange(SEQ_ROWS, dtype=jnp.int32)
    single = row_ids % SEQS == chosen[row_ids // SEQS]
    return jnp.where(single[:, None], 0, seg_ids).astype(jnp.int32)


def block_scale(stream_key, dims, cuts, least, high):
    level, own = 1.0, jax.random.fold_in(stream_key, 6)
    for dim, parts in cuts:
        draws = jnp.exp(jax.random.uniform(jax.random.fold_in(own, dim), (parts,), jnp.float32, least / len(cuts), high / len(cuts)))
        level = level * jnp.repeat(draws, dims[dim] // parts).reshape([-1 if axis == dim else 1 for axis in range(len(dims))])
    return level


def normal_values(own_key, shape, deviation, limit, pieces=(), held_as=jnp.bfloat16):
    entries = jax.random.normal(own_key, shape, jnp.float32) * deviation
    if len(pieces) > 0:
        entries = block_scale(own_key, shape, pieces, -0.22, 0.18) * entries
    return jnp.clip(entries, min=-limit, max=limit).astype(held_as)


def setup_inputs(seed: int = 0) -> dict:
    key_list = jax.random.split(jax.random.key(seed), 10)
    tokens = normal_values(key_list[0], (SEQ_ROWS, LENGTH, MODEL_WIDTH), 1.0, 6.0, ((0, 8), (1, 4)))
    segments = draw_segments(jax.random.fold_in(key_list[9], 71), 0)
    cotangent = normal_values(key_list[2], (SEQ_ROWS, LENGTH, MODEL_WIDTH), 1.0, 6.0, ((0, 8), (1, 4)))
    attn_gain = jnp.clip(1.0 + 0.18 * jax.random.normal(key_list[3], (MODEL_WIDTH,), jnp.float32), 0.099609375, 1.8984375).astype(jnp.bfloat16)
    mlp_gain = jnp.clip(1.0 + 0.18 * jax.random.normal(key_list[4], (MODEL_WIDTH,), jnp.float32), 0.099609375, 1.8984375).astype(jnp.bfloat16)
    query_key_value_weight = normal_values(key_list[5], (MODEL_WIDTH * (QUERY_HEADS + 2 * KEY_VALUE_HEADS) * HEAD_WIDTH,), MODEL_WIDTH ** -0.5, 0.1875, ((0, 32),))
    w_out = normal_values(key_list[6], (QUERY_HEADS * HEAD_WIDTH * MODEL_WIDTH,), (max(QUERY_HEADS * HEAD_WIDTH // 64, 1)) ** -0.5, 1.5, ((0, 32),))
    w_gate_up = normal_values(key_list[7], (2 * MODEL_WIDTH * FF,), MODEL_WIDTH ** -0.5, 0.1875, ((0, 32),))
    w_down = normal_values(key_list[8], (FF * MODEL_WIDTH,), FF ** -0.5, 0.125, ((0, 32),))
    return dict(tokens=tokens, segments=segments, cotangent=cotangent, attn_gain=attn_gain, mlp_gain=mlp_gain, query_key_value_weight=query_key_value_weight, w_out=w_out, w_gate_up=w_gate_up, w_down=w_down)


EPS = 1e-05
ROPE_BASE = 100000.0

@jax.custom_vjp
def low(v):
    return lax.optimization_barrier(v.astype(jnp.bfloat16)).astype(jnp.float32)

@jax.custom_vjp
def low_back(v):
    return v

def low_keep(v):
    return (low(v), None)

def low_pass(kept, grad):
    return (grad,)

def back_keep(v):
    return (v, None)

def back_low(kept, grad):
    return (low(grad),)
low.defvjp(low_keep, low_pass)
low_back.defvjp(back_keep, back_low)

def matmul(left, right):
    return jnp.einsum('...d,de->...e', left, right, precision=lax.Precision.HIGHEST)

def rms_norm(value, gain):
    factor = lax.rsqrt(lax.optimization_barrier(jnp.mean(value * value, axis=-1, keepdims=True)) + EPS)
    return value * factor * gain

def rotate(heads, cosine, sine):
    half = heads.shape[-1] // 2
    first = heads[..., :half]
    second = heads[..., half:]
    return jnp.concatenate([first * cosine - second * sine, second * cosine + first * sine], axis=-1)

def attend(item):
    query_rows, keys, values, seg_row = item
    length_total = seg_row.shape[0]
    grouped_heads = query_rows.reshape(length_total, KEY_VALUE_HEADS, QUERY_HEADS // KEY_VALUE_HEADS, HEAD_WIDTH)
    scores = jnp.einsum('qkgd,lkd->kgql', grouped_heads, keys, precision=lax.Precision.HIGHEST) * HEAD_WIDTH ** (-0.5)
    scores = low_back(scores)
    index = jnp.arange(length_total, dtype=jnp.int32)
    valid = (seg_row[:, None] == seg_row[None, :]) & (index[None, :] <= index[:, None])
    scores = jnp.where(valid[None, None], scores, -1e+30)
    probs = jax.nn.softmax(scores, axis=-1)
    mixed = jnp.einsum('kgql,lkd->qkgd', low(probs), values, precision=lax.Precision.HIGHEST)
    return mixed.reshape(length_total, QUERY_HEADS * HEAD_WIDTH)

def forward(x, gain_one, gain_two, query_key_value_weight, w_out, w_gate_up, w_down, segments):
    row_count, length_total = segments.shape
    query_key_value_matrix = query_key_value_weight.reshape(MODEL_WIDTH, (QUERY_HEADS + 2 * KEY_VALUE_HEADS) * HEAD_WIDTH)
    wout = w_out.reshape(QUERY_HEADS * HEAD_WIDTH, MODEL_WIDTH)
    wgu = w_gate_up.reshape(MODEL_WIDTH, 2 * FF)
    wdown = w_down.reshape(FF, MODEL_WIDTH)
    position = (jnp.arange(length_total, dtype=jnp.int32)[None, :] - segments).astype(jnp.float32)
    inverse = ROPE_BASE ** (-2.0 * jnp.arange(HEAD_WIDTH // 2, dtype=jnp.float32) / HEAD_WIDTH)
    angle = position[:, :, None, None] * inverse
    cosine = jnp.cos(angle)
    sine = jnp.sin(angle)
    normed1 = low(rms_norm(x, gain_one))
    projected = low_back(matmul(normed1, query_key_value_matrix))
    query0 = projected[..., :QUERY_HEADS * HEAD_WIDTH].reshape(row_count, length_total, QUERY_HEADS, HEAD_WIDTH)
    key_initial = projected[..., QUERY_HEADS * HEAD_WIDTH:(QUERY_HEADS + KEY_VALUE_HEADS) * HEAD_WIDTH].reshape(row_count, length_total, KEY_VALUE_HEADS, HEAD_WIDTH)
    value_initial = projected[..., (QUERY_HEADS + KEY_VALUE_HEADS) * HEAD_WIDTH:].reshape(row_count, length_total, KEY_VALUE_HEADS, HEAD_WIDTH)
    query_rows = low(rotate(query0, cosine, sine))
    keys = low(rotate(key_initial, cosine, sine))
    values = low(value_initial)
    mixed = lax.map(jax.checkpoint(attend), (query_rows, keys, values, segments))
    mixed = low(low_back(mixed))
    hidden = x + low_back(matmul(mixed, wout))
    normed2 = low(rms_norm(hidden, gain_two))
    gate_up = low_back(matmul(normed2, wgu))
    gate = gate_up[..., :FF]
    upper = gate_up[..., FF:]
    act = low(jax.nn.silu(gate) * upper)
    return hidden + matmul(act, wdown)

def reference(tokens, segments, cotangent, attn_gain, mlp_gain, query_key_value_weight, w_out, w_gate_up, w_down):
    inputs = (tokens.astype(jnp.float32), attn_gain.astype(jnp.float32), mlp_gain.astype(jnp.float32), query_key_value_weight.astype(jnp.float32), w_out.astype(jnp.float32), w_gate_up.astype(jnp.float32), w_down.astype(jnp.float32))

    def whole(x, gain_one, gain_two, query_key_value_matrix, wout, wgu, wdown):
        return forward(x, gain_one, gain_two, query_key_value_matrix, wout, wgu, wdown, segments)
    result, pullback = jax.vjp(whole, *inputs)
    grads = pullback(cotangent.astype(jnp.float32))
    return (result.astype(jnp.bfloat16), grads[0], grads[1], grads[2], grads[3], grads[4], grads[5], grads[6])
```

```python
import functools

import jax
import jax.numpy as jnp
from jax import lax
from jax.experimental import pallas as pl
from jax.experimental.pallas import tpu as pltpu
from jax.sharding import PartitionSpec as P

QUERY_HEADS = 15
KEY_VALUE_HEADS = 5
HEAD_WIDTH = 64
GROUPS = QUERY_HEADS // KEY_VALUE_HEADS

EPS = 1e-05
ROPE_BASE = 100000.0
SCALE = HEAD_WIDTH ** (-0.5)
SCALE_LOG2 = SCALE * 1.4426950408889634
KEY_TILE = 512
QUERY_TILE = 512
FORWARD_QUERY_TILE = 512

F32 = jnp.float32
BF16 = jnp.bfloat16


def rotate(heads, cosine, sine):
    half = heads.shape[2] // 2
    first = heads[:, :, :half]
    second = heads[:, :, half:]
    return jnp.concatenate(
        [first * cosine - second * sine, second * cosine + first * sine], axis=2
    )


def norm_back(value, factor, gain, d_normed):
    gain_part = jnp.sum(d_normed * value * factor, axis=(0, 1))
    scaled = d_normed * gain
    d_value = factor * scaled - value * factor * factor * factor * jnp.mean(
        scaled * value, axis=-1, keepdims=True
    )
    return (d_value, gain_part)


def gather_weight(flat, width):
    if flat.shape[0] % width == 0:
        return lax.all_gather(flat.reshape(-1, width), ("dp", "seq"), axis=0, tiled=True)
    return lax.all_gather(flat, ("dp", "seq"), axis=0, tiled=True).reshape(-1, width)


def dot(left, right, dims):
    return lax.dot_general(left, right, (dims, ((), ())), preferred_element_type=F32)


def valid_keys(index, seg, q_index, me, block, tile, q_tile):
    keys = index * tile + lax.broadcasted_iota(jnp.int32, (tile, q_tile), 0)
    first = me * block + q_index * q_tile
    query = first + lax.broadcasted_iota(jnp.int32, (1, q_tile), 1)
    return (keys >= seg) & (keys <= query)


def key_range(low_ref, q_index, me, block, tile, q_tile):
    return low_ref[q_index], (me * block + (q_index + 1) * q_tile + tile - 1) // tile


def attend_kernel(block, tile, q_tile, me_ref, low_ref, q_ref, kv_ref, seg_ref, out_ref, lse_ref):
    q_index = pl.program_id(1)
    me = me_ref[0]
    parts = block // tile
    seg = seg_ref[...]

    def step(index, state):
        slot = me - index // parts
        part = lax.rem(index, parts)
        where = pl.ds(pl.multiple_of(part * tile, tile), tile)
        keys = kv_ref[slot, 0, 0, :, where]
        values = kv_ref[slot, 1, 0, :, where]
        valid = valid_keys(index, seg, q_index, me, block, tile, q_tile)
        out = []
        for head in range(GROUPS):
            top, total, mixed = state[head]
            scores = dot(keys, q_ref[head], ((0,), (0,))) * SCALE_LOG2
            scores = jnp.where(valid, scores, -1e30)
            new_top = jnp.maximum(top, jnp.max(scores, axis=0, keepdims=True))
            probs = jnp.exp2(scores - new_top)
            shrink = jnp.exp2(top - new_top)
            total = total * shrink + jnp.sum(probs, axis=0, keepdims=True)
            mixed = mixed * shrink + dot(values, probs.astype(BF16), ((1,), (0,)))
            out.append((new_top, total, mixed))
        return tuple(out)

    first = (
        jnp.full((1, q_tile), -1e30, F32),
        jnp.zeros((1, q_tile), F32),
        jnp.zeros((HEAD_WIDTH, q_tile), F32),
    )
    begin, end = key_range(low_ref, q_index, me, block, tile, q_tile)
    state = lax.fori_loop(begin, end, step, (first,) * GROUPS)
    for head in range(GROUPS):
        top, total, mixed = state[head]
        out_ref[head] = (mixed / total).astype(BF16)
        lse_ref[head] = top + jnp.log2(total)


def attend_back_kernel(
    block, tile, q_tile, steps, me_ref, low_ref, q_ref, kv_ref, seg_ref, out_ref, lse_ref, d_out_ref,
    d_q_ref, d_kv_ref, sums
):
    q_index = pl.program_id(1)
    me = me_ref[0]
    parts = block // tile
    seg = seg_ref[...]

    @pl.when(q_index == 0)
    def _():
        sums[...] = jnp.zeros_like(sums)

    inner = [
        jnp.sum(d_out_ref[head].astype(F32) * out_ref[head].astype(F32), axis=0, keepdims=True)
        for head in range(GROUPS)
    ]

    def step(index, state):
        slot = me - index // parts
        part = lax.rem(index, parts)
        where = pl.ds(pl.multiple_of(part * tile, tile), tile)
        keys = kv_ref[slot, 0, 0, :, where]
        values = kv_ref[slot, 1, 0, :, where]
        valid = valid_keys(index, seg, q_index, me, block, tile, q_tile)
        out = []
        d_key = jnp.zeros((HEAD_WIDTH, tile), F32)
        d_value = jnp.zeros((HEAD_WIDTH, tile), F32)
        for head in range(GROUPS):
            query = q_ref[head]
            d_out = d_out_ref[head]
            scores = dot(keys, query, ((0,), (0,))) * SCALE_LOG2
            probs = jnp.exp2(jnp.where(valid, scores, -1e30) - lse_ref[head])
            d_probs = dot(values, d_out, ((0,), (0,)))
            d_scores = (probs * (d_probs - inner[head])).astype(BF16)
            out.append(state[head] + dot(keys, d_scores, ((1,), (0,))))
            d_key += dot(query, d_scores, ((1,), (1,)))
            d_value += dot(d_out, probs.astype(BF16), ((1,), (1,)))
        sums[slot, 0, :, where] += d_key
        sums[slot, 1, :, where] += d_value
        return tuple(out)

    begin, end = key_range(low_ref, q_index, me, block, tile, q_tile)
    state = lax.fori_loop(
        begin, end, step, (jnp.zeros((HEAD_WIDTH, q_tile), F32),) * GROUPS
    )
    for head in range(GROUPS):
        d_q_ref[head] = (state[head] * SCALE).astype(d_q_ref.dtype)

    @pl.when(q_index == steps - 1)
    def _():
        d_kv_ref[:, 0, 0] = (sums[:, 0] * SCALE).astype(d_kv_ref.dtype)
        d_kv_ref[:, 1, 0] = sums[:, 1].astype(d_kv_ref.dtype)


def low_tiles(seg, tile, q_tile):
    return seg[0, ::q_tile] // tile


def attention_specs(slots, block, tile):
    heads = pl.BlockSpec((GROUPS, HEAD_WIDTH, tile), lambda g, q, *_: (g, 0, q))
    kv = pl.BlockSpec((slots, 2, 1, HEAD_WIDTH, block), lambda g, q, *_: (0, 0, g, 0, 0))
    seg = pl.BlockSpec((1, tile), lambda g, q, *_: (0, q))
    lse = pl.BlockSpec((GROUPS, 1, tile), lambda g, q, *_: (g, 0, q))
    return heads, kv, seg, lse


def attend(me, query, kv, seg):
    slots, block = kv.shape[0], query.shape[-1]
    tile, q_tile = min(KEY_TILE, block), min(FORWARD_QUERY_TILE, block)
    low = low_tiles(seg, tile, q_tile)
    heads, kv_spec, seg_spec, lse = attention_specs(slots, block, q_tile)
    work = QUERY_HEADS * block * slots * block
    return pl.pallas_call(
        functools.partial(attend_kernel, block, tile, q_tile),
        grid_spec=pltpu.PrefetchScalarGridSpec(
            num_scalar_prefetch=2,
            grid=(KEY_VALUE_HEADS, block // q_tile),
            in_specs=[heads, kv_spec, seg_spec],
            out_specs=[heads, lse],
        ),
        out_shape=[
            jax.ShapeDtypeStruct(query.shape, BF16),
            jax.ShapeDtypeStruct((QUERY_HEADS, 1, block), F32),
        ],
        compiler_params=pltpu.CompilerParams(vmem_limit_bytes=40 * 2**20),
        cost_estimate=pl.CostEstimate(
            flops=16 * work * HEAD_WIDTH, bytes_accessed=8 * 2**20, transcendentals=work
        ),
        name="attend",
    )(me, low, query, kv, seg)


def attend_back(me, query, kv, seg, attn, lse_rows, d_attn):
    slots, block = kv.shape[0], query.shape[-1]
    tile, q_tile = min(KEY_TILE, block), min(QUERY_TILE, block)
    low = low_tiles(seg, tile, q_tile)
    heads, kv_spec, seg_spec, lse = attention_specs(slots, block, q_tile)
    work = QUERY_HEADS * block * slots * block
    return pl.pallas_call(
        functools.partial(attend_back_kernel, block, tile, q_tile, block // q_tile),
        grid_spec=pltpu.PrefetchScalarGridSpec(
            num_scalar_prefetch=2,
            grid=(KEY_VALUE_HEADS, block // q_tile),
            in_specs=[heads, kv_spec, seg_spec, heads, lse, heads],
            out_specs=[heads, kv_spec],
            scratch_shapes=[pltpu.VMEM((slots, 2, HEAD_WIDTH, block), F32)],
        ),
        out_shape=[
            jax.ShapeDtypeStruct(query.shape, F32),
            jax.ShapeDtypeStruct(kv.shape, BF16),
        ],
        compiler_params=pltpu.CompilerParams(vmem_limit_bytes=40 * 2**20),
        cost_estimate=pl.CostEstimate(
            flops=40 * work * HEAD_WIDTH, bytes_accessed=16 * 2**20, transcendentals=work
        ),
        name="attend_back",
    )(me, low, query, kv, seg, attn, lse_rows, d_attn)


def from_before(own, slots):
    held = [own]
    for slot in range(1, slots):
        pairs = [(i, i + slot) for i in range(slots - slot)]
        held.append(lax.ppermute(own, "seq", pairs))
    return jnp.stack(held)


def sum_to_owner(parts, slots):
    total = parts[0].astype(F32)
    for slot in range(1, slots):
        pairs = [(i + slot, i) for i in range(slots - slot)]
        total += lax.ppermute(parts[slot], "seq", pairs).astype(F32)
    return total


def scatter_sum(grad, dp, seq):
    rows, width = grad.shape
    part = lax.psum_scatter(grad, "dp", scatter_dimension=0, tiled=True)
    if (rows // dp) % seq != 0:
        part = part.reshape(seq, -1)
    else:
        part = part.reshape(seq, rows // dp // seq, width)
    owned = lax.psum_scatter(part, "seq", scatter_dimension=0, tiled=False)
    return owned.astype(F32).reshape(-1)


def local(
    dp,
    slots,
    tokens,
    segments,
    cotangent,
    attn_gain,
    mlp_gain,
    query_key_value_weight,
    w_out,
    w_gate_up,
    w_down,
):
    seqs, block, width = tokens.shape
    me = lax.axis_index("seq")
    start = me * block
    qkv_width = (QUERY_HEADS + 2 * KEY_VALUE_HEADS) * HEAD_WIDTH
    hidden_units = w_down.shape[0] * dp * slots // width
    w_qkv = gather_weight(query_key_value_weight, qkv_width)
    wout = gather_weight(w_out, width)
    wgu = gather_weight(w_gate_up, 2 * hidden_units)
    wdown = gather_weight(w_down, width)
    gain_one = attn_gain.astype(F32)
    gain_two = mlp_gain.astype(F32)
    x = tokens.astype(F32)
    rms_one = lax.rsqrt(jnp.mean(x * x, axis=-1, keepdims=True) + EPS)
    normed1 = (x * rms_one * gain_one).astype(BF16)
    projected = jnp.einsum("de,scd->sec", w_qkv, normed1, preferred_element_type=F32)
    projected = projected.reshape(seqs, -1, HEAD_WIDTH, block)
    places = start + jnp.arange(block, dtype=jnp.int32)
    seg_local = lax.dynamic_slice_in_dim(segments, start, block, 1)
    position = (places[None, :] - seg_local).astype(F32)
    inverse = ROPE_BASE ** (-2.0 * jnp.arange(HEAD_WIDTH // 2, dtype=F32) / HEAD_WIDTH)
    angle = inverse[None, None, :, None] * position[:, None, None, :]
    cosine = jnp.cos(angle)
    sine = jnp.sin(angle)
    turned = rotate(projected[:, : QUERY_HEADS + KEY_VALUE_HEADS], cosine, sine).astype(BF16)
    query = turned[:, :QUERY_HEADS]
    kv_own = jnp.stack(
        [turned[:, QUERY_HEADS:], projected[:, QUERY_HEADS + KEY_VALUE_HEADS :].astype(BF16)],
        axis=1,
    )
    me_row = me.astype(jnp.int32).reshape(1)

    kv, attn_rows, lse_rows = [], [], []
    for row in range(seqs):
        own = kv_own[row]
        if row > 0:
            own, kv[-1] = lax.optimization_barrier((own, kv[-1]))
        kv.append(from_before(own, slots))
    for row in range(seqs):
        mixed, lse = attend(me_row, query[row], kv[row], seg_local[row : row + 1])
        attn_rows.append(mixed)
        lse_rows.append(lse)
    attn = jnp.stack(attn_rows).reshape(seqs, QUERY_HEADS * HEAD_WIDTH, block)

    hidden = x + jnp.einsum("sec,ed->scd", attn, wout, preferred_element_type=F32)
    rms_two = lax.rsqrt(jnp.mean(hidden * hidden, axis=-1, keepdims=True) + EPS)
    normed2 = (hidden * rms_two * gain_two).astype(BF16)
    gate_up = jnp.einsum("scd,de->sce", normed2, wgu, preferred_element_type=F32)
    gate = gate_up[..., :hidden_units]
    upper = gate_up[..., hidden_units:]
    silu_gate = jax.nn.silu(gate)
    act = (silu_gate * upper).astype(BF16)
    output = (
        hidden + jnp.einsum("scf,fd->scd", act, wdown, preferred_element_type=F32)
    ).astype(BF16)
    grad_down = jnp.einsum("scf,scd->fd", act, cotangent, preferred_element_type=F32)
    grad_down, dy = lax.optimization_barrier((grad_down.astype(BF16), cotangent))
    down_owned = scatter_sum(grad_down, dp, slots)
    d_act = jnp.einsum("scd,fd->scf", dy, wdown, preferred_element_type=F32)
    sigma = jax.nn.sigmoid(gate)
    d_gate = d_act * upper * sigma * (1.0 + gate * (1.0 - sigma))
    d_upper = d_act * silu_gate
    d_gate_up = jnp.concatenate([d_gate, d_upper], axis=-1).astype(BF16)
    grad_gate_up = jnp.einsum("scd,sce->de", normed2, d_gate_up, preferred_element_type=F32)
    grad_gate_up, d_gu = lax.optimization_barrier((grad_gate_up.astype(BF16), d_gate_up))
    gate_up_owned = scatter_sum(grad_gate_up, dp, slots)
    d_normed2 = jnp.einsum("sce,de->scd", d_gu, wgu, preferred_element_type=F32)
    d_from_norm, grad_gain_two = norm_back(hidden, rms_two, gain_two, d_normed2)
    d_hidden = cotangent.astype(F32) + d_from_norm
    d_hid_low = d_hidden.astype(BF16)
    d_attn = jnp.einsum("ed,scd->sec", wout, d_hid_low, preferred_element_type=F32).astype(BF16)
    d_attn = d_attn.reshape(seqs, QUERY_HEADS, HEAD_WIDTH, block)
    grad_out = jnp.einsum("sec,scd->ed", attn, d_hid_low, preferred_element_type=F32)
    grad_out, d_attn = lax.optimization_barrier((grad_out.astype(BF16), d_attn))
    out_owned = scatter_sum(grad_out, dp, slots)

    d_query, d_kv = [], []
    for row in range(seqs):
        d_q_row, d_kv_row = attend_back(
            me_row,
            query[row],
            kv[row],
            seg_local[row : row + 1],
            attn_rows[row],
            lse_rows[row],
            d_attn[row],
        )
        d_query.append(d_q_row)
        d_kv.append(sum_to_owner(d_kv_row, slots))
    d_query = jnp.stack(d_query)
    d_kv = jnp.stack(d_kv)
    d_turned = rotate(jnp.concatenate([d_query, d_kv[:, 0]], axis=1), cosine, -sine)
    d_proj = (
        jnp.concatenate([d_turned, d_kv[:, 1]], axis=1).reshape(seqs, -1, block).astype(BF16)
    )
    grad_qkv = jnp.einsum("scd,sec->de", normed1, d_proj, preferred_element_type=F32)
    qkv_owned = scatter_sum(grad_qkv.astype(BF16), dp, slots)
    d_normed1 = jnp.einsum("sec,de->scd", d_proj, w_qkv, preferred_element_type=F32)
    d_from_first, grad_gain_one = norm_back(x, rms_one, gain_one, d_normed1)
    input_grad = d_hidden + d_from_first
    gain_one_total, gain_two_total = lax.psum((grad_gain_one, grad_gain_two), ("dp", "seq"))
    return (
        output,
        input_grad,
        gain_one_total,
        gain_two_total,
        qkv_owned,
        out_owned,
        gate_up_owned,
        down_owned,
    )


def solution(mesh):
    rows = P("dp", "seq", None)
    flat = P(("dp", "seq"))
    return jax.shard_map(
        functools.partial(local, mesh.shape["dp"], mesh.shape["seq"]),
        mesh=mesh,
        in_specs=(rows, P("dp", None), rows, P(), P(), flat, flat, flat, flat),
        out_specs=(rows, rows, P(), P(), flat, flat, flat, flat),
        check_vma=False,
    )
```
